32 devices in a mesh: gx: 4 (over x, core), gy: 8 (over z, y).
Axes of the slice: x: 2, y: 2, z: 4, core: 2. Of those that a mesh axis runs over, the one named last changes fastest.
Arguments:
- coefficients: float32 [3, 16, 128, 128], P(None, 'gx', 'gy'), may hold values from -3 to 3
- fractions: float32 [3, 65536], P(None, ('gx', 'gy')), may hold values from 0 to 1
- targets: float32 [3, 65536], P(None, ('gx', 'gy')), may hold values from -6 to 6
- block_cell: int32 [512], P(('gx', 'gy')), may hold values from 0 to 8191
- block_fill: int32 [512], P(('gx', 'gy')), may hold values from 0 to 128, as said below
Outputs:
- fitted: float32 [3, 16, 128, 128], P(None, 'gx', 'gy')
- losses: float32 [4], replicated
The draws below stay inside these ranges and needn't reach their ends.
Inputs may be any that keep to these rules, and one draw needn't show every extreme that they name: `block_fill`: in each brick's 16 slots the live blocks come first and the empty ones (fill 0) last; every brick's first block holds 128 samples, and the brick with the most live blocks has all slots live.
All inputs are finite; a program needn't handle non-finite values.
Results may differ from the reference program's by a relative error of at most 0.0001.
Values sent between devices are 32-bit elements; how exact they have to be, the bound alone decides.
A program may use at most 64 MiB of HBM per device.

```python
import math
import jax
import jax.numpy as jnp
from jax import lax

CX = 4
CY = 16
NZ = 128
BLK_DEV = 16
SAMPLES = 128
ITERS = 4
BRICKS_X = 4
BRICKS_Y = 8
NX = 16
NY = 128
CELLS_DEV = 8192
NBLK = 512
NSAMP = 65536
N_GY = 8


def draw_block_fill(key, part):
    key = jax.random.fold_in(key, 7)
    positions = jnp.arange(NBLK, dtype=jnp.int32)
    device = positions // BLK_DEV
    within = positions % BLK_DEV
    column = device // BRICKS_Y
    live_count = BLK_DEV // 4 + (BLK_DEV - BLK_DEV // 4) * column // max(BRICKS_X - 1, 1)
    live_count = jnp.maximum(live_count, 1)
    fill_sizes = jax.random.randint(key, (NBLK,), 1, SAMPLES + 1)
    fill_sizes = jnp.where(within == 0, SAMPLES, fill_sizes)
    return jnp.where(within < live_count, fill_sizes, 0).astype(jnp.int32)


def set_ends(entries, rng, smallest, top_value):
    place = [jax.random.randint(jax.random.fold_in(rng, axis), (), 0, length) for axis, length in enumerate(entries.shape)]
    main_axis = entries.shape.index(max(entries.shape))
    neighbour = place[:main_axis] + [(place[main_axis] + 1) % entries.shape[main_axis]] + place[main_axis + 1:]
    return entries.at[tuple(place)].set(smallest).at[tuple(neighbour)].set(top_value)


def block_scale(key, shape, split, least, largest):
    gain = 1.0
    for position, blocks in split:
        steps = jax.random.uniform(jax.random.fold_in(jax.random.fold_in(key, 6), position), (blocks,), jnp.float32, least / len(split), largest / len(split))
        gain = gain * jnp.repeat(jnp.exp(steps), shape[position] // blocks).reshape((-1,) + (1,) * (len(shape) - 1 - position))
    return gain


def normal_values(own_key, dims, scale, limit, pieces=(), held_as=jnp.bfloat16):
    gain = block_scale(own_key, dims, pieces, -0.22, 0.18) if pieces else 1.0
    array = jax.random.normal(own_key, dims, jnp.float32) * scale * gain
    return jnp.minimum(jnp.maximum(array, -limit), limit).astype(held_as)


def setup_inputs(seed: int = 0) -> dict:
    keys = jax.random.split(jax.random.key(seed), 6)
    coefficients = normal_values(keys[0], (3, NX, NY, NZ), 0.5, 3.0, ((1, 4), (2, 8)), jnp.float32)
    fractions = jnp.clip(1.0 * jax.random.uniform(keys[1], (3, NSAMP), jnp.float32) ** block_scale(keys[1], (3, NSAMP), ((1, 32),), -0.2, 0.2), 0.0, 1.0)
    targets = normal_values(keys[2], (3, NSAMP), 1.0, 6.0, ((1, 32),), jnp.float32)
    block_cell = set_ends(jax.random.randint(keys[3], (NBLK,), 0, CELLS_DEV), jax.random.fold_in(keys[3], 1), 0, CELLS_DEV - 1).astype(jnp.int32)
    block_fill = draw_block_fill(jax.random.fold_in(keys[5], 71), 0)
    return {"coefficients": coefficients, "fractions": fractions, "targets": targets, "block_cell": block_cell, "block_fill": block_fill}


penalty_weight = 0.5
learn_rate = 0.05
beta_one = 0.9
beta_two = 0.999
adam_eps = 0.1

def spline_weights(u):
    one_minus = 1.0 - u
    return jnp.stack([one_minus ** 3 / 6.0, (3.0 * u ** 3 - 6.0 * u ** 2 + 4.0) / 6.0, (-3.0 * u ** 3 + 3.0 * u ** 2 + 3.0 * u + 1.0) / 6.0, u ** 3 / 6.0])

def tensor_basis(fraction):
    full = jnp.einsum('ags,bgs,cgs->gsabc', spline_weights(fraction[0]), spline_weights(fraction[1]), spline_weights(fraction[2]), precision=lax.Precision.HIGHEST)
    return full.reshape(full.shape[0], full.shape[1], 64)

def node_offsets():
    nodes = jnp.arange(64, dtype=jnp.int32)
    return (nodes // 16, nodes // 4 % 4, nodes % 4)

def divergence_parts(coef):
    padc = jnp.pad(coef, ((0, 0), (1, 1), (1, 1), (1, 1)))
    divergence = (padc[0, 2:, 1:-1, 1:-1] - padc[0, :-2, 1:-1, 1:-1] + padc[1, 1:-1, 2:, 1:-1] - padc[1, 1:-1, :-2, 1:-1] + padc[2, 1:-1, 1:-1, 2:] - padc[2, 1:-1, 1:-1, :-2]) / 2.0
    padd = jnp.pad(divergence, 1)
    grad_div = jnp.stack([penalty_weight * (padd[:-2, 1:-1, 1:-1] - padd[2:, 1:-1, 1:-1]), penalty_weight * (padd[1:-1, :-2, 1:-1] - padd[1:-1, 2:, 1:-1]), penalty_weight * (padd[1:-1, 1:-1, :-2] - padd[1:-1, 1:-1, 2:])])
    return (jnp.sum(divergence * divergence), grad_div)

def reference(coefficients, fractions, targets, block_cell, block_fill):
    ncells = NX * NY * NZ
    grand_total = jnp.sum(block_fill).astype(jnp.float32)
    data_scale = ncells / grand_total
    positions = jnp.arange(NBLK, dtype=jnp.int32)
    device = positions // BLK_DEV
    column = device // N_GY
    row_no = device % N_GY
    cell_x = (column * CX + block_cell // (CY * NZ)).astype(jnp.int32)
    cell_y = (row_no * CY + block_cell // NZ % CY).astype(jnp.int32)
    cell_z = (block_cell % NZ).astype(jnp.int32)
    group = math.gcd(NBLK, 256)
    rounds = NBLK // group
    fraction = jnp.moveaxis(fractions.reshape(3, rounds, group, SAMPLES), 1, 0)
    target = jnp.moveaxis(targets.reshape(3, rounds, group, SAMPLES), 1, 0)
    alive = (jnp.arange(SAMPLES, dtype=jnp.int32)[None, :] < block_fill[:, None]).astype(jnp.float32)
    items = (cell_x.reshape(rounds, group), cell_y.reshape(rounds, group), cell_z.reshape(rounds, group), fraction, target, alive.reshape(rounds, group, SAMPLES))
    off_x, off_y, off_z = node_offsets()

    def evaluate(coef):
        padded = jnp.pad(coef, ((0, 0), (2, 2), (2, 2), (2, 2)))

        def take_patch(a_pos, b_pos, c_pos):
            return lax.dynamic_slice(padded, (jnp.int32(0), a_pos + 1, b_pos + 1, c_pos + 1), (3, 4, 4, 4))

        def one_group(carry, item):
            grad_pad, data_sq = carry
            pos_x, pos_y, pos_z, frac, tgt, live = item
            patches = jax.vmap(take_patch)(pos_x, pos_y, pos_z).reshape(group, 3, 64)
            basis_mat = tensor_basis(frac)
            predicted = jnp.einsum('gsn,gcn->cgs', basis_mat, patches, precision=lax.Precision.HIGHEST)
            misfit = (predicted - tgt) * live[None]
            data_sq = data_sq + jnp.sum(misfit * misfit)
            term = 2.0 * data_scale * jnp.einsum('gsn,cgs->cgn', basis_mat, misfit, precision=lax.Precision.HIGHEST)
            grad_pad = grad_pad.at[:, pos_x[:, None] + 1 + off_x, pos_y[:, None] + 1 + off_y, pos_z[:, None] + 1 + off_z].add(term)
            return ((grad_pad, data_sq), None)
        start = (jnp.zeros(padded.shape, jnp.float32), jnp.float32(0.0))
        (grad_pad, data_sq), unused = lax.scan(one_group, start, items)
        spread, grad_div = divergence_parts(coef)
        gradient = grad_pad[:, 2:-2, 2:-2, 2:-2] + grad_div
        return (data_sq, spread, gradient)
    current = coefficients
    moment = jnp.zeros_like(coefficients)
    second = jnp.zeros_like(coefficients)
    history = []
    for iteration in range(ITERS):
        data_sq, spread, gradient = evaluate(current)
        history.append(data_sq / grand_total + penalty_weight * spread / ncells)
        moment = beta_one * moment + (1.0 - beta_one) * gradient
        second = beta_two * second + (1.0 - beta_two) * gradient * gradient
        corr_one = 1.0 - beta_one ** (iteration + 1)
        corr_two = 1.0 - beta_two ** (iteration + 1)
        current = current - learn_rate * (moment / corr_one) / (jnp.sqrt(second / corr_two) + adam_eps)
    return (current, jnp.stack(history))
```

```python
import functools

import jax
import jax.numpy as jnp
from jax import lax
from jax.experimental import pallas as pl
from jax.experimental.pallas import tpu as pltpu
from jax.sharding import PartitionSpec as P

ITERS = 4

penalty_weight = 0.5
learn_rate = 0.05
beta_one = 0.9
beta_two = 0.999
adam_eps = 0.1

MESH = pl.DeviceIdType.MESH
DIRS = ((1, 0), (-1, 0), (0, 1), (0, -1), (1, 1), (-1, 1), (1, -1), (-1, -1))
F32 = jnp.float32
BF16 = jnp.bfloat16


def cubic(u):
    one = 1.0 - u
    return (
        one * one * one / 6.0,
        (3.0 * u * u * u - 6.0 * u * u + 4.0) / 6.0,
        (-3.0 * u * u * u + 3.0 * u * u + 3.0 * u + 1.0) / 6.0,
        u * u * u / 6.0,
    )


def split(x):
    hi = x.astype(BF16)
    lo = (x - hi.astype(F32)).astype(BF16)
    return hi, lo


def mm(a, b):
    return jnp.dot(a, b, preferred_element_type=F32)


def mm_nt(a, b):
    return lax.dot_general(a, b, (((1,), (1,)), ((), ())), preferred_element_type=F32)


def iota(shape, dim):
    return lax.broadcasted_iota(jnp.int32, shape, dim)


def kernel(
    nx, ny, cell_ref, fill_ref, coef_ref, frac_ref, targ_ref, out_ref, loss_ref,
    cur, mom, sec, grad, total, wt_hi, wt_lo, uv, sel, sel_t, term, sy, sc, rx, ry, rc,
    red_src, red_x, red_y, send_sem, recv_sem, rs_x, rr_x, rs_y, rr_y,
):
    comps, cx, cy, nz = coef_ref.shape
    blocks = cell_ref.shape[0]
    ex, ey = cx + 3, cy + 8
    rows = ex * ey
    gx, gy = lax.axis_index("gx"), lax.axis_index("gy")
    ncells = float(cx * nx * cy * ny * nz)
    low_rows = (ey - 1, 0, 1)
    high_rows = (cy - 1, cy, cy + 1)

    def here(d, sign):
        x, y = gx + sign * d[0], gy + sign * d[1]
        return (x >= 0) & (x < nx) & (y >= 0) & (y < ny)

    can_send = [here(d, 1) for d in DIRS]
    can_recv = [here(d, -1) for d in DIRS]

    barrier = pltpu.get_barrier_semaphore()
    for n, d in enumerate(DIRS):
        @pl.when(can_send[n])
        def _():
            pl.semaphore_signal(barrier, inc=1, device_id=(gx + d[0], gy + d[1]), device_id_type=MESH)
    for k in range(1, nx):
        pl.semaphore_signal(barrier, inc=1, device_id=(lax.rem(gx + k, nx), gy), device_id_type=MESH)
    for k in range(1, ny):
        pl.semaphore_signal(barrier, inc=1, device_id=(gx, lax.rem(gy + k, ny)), device_id_type=MESH)

    def reduce_copy(kind, stage, k):
        if stage == 0:
            return pltpu.make_async_remote_copy(
                src_ref=red_src.at[kind, 0], dst_ref=red_x.at[kind, k - 1],
                send_sem=rs_x.at[kind, k - 1], recv_sem=rr_x.at[kind, k - 1],
                device_id=(lax.rem(gx + k, nx), gy), device_id_type=MESH)
        return pltpu.make_async_remote_copy(
            src_ref=red_src.at[kind, 1], dst_ref=red_y.at[kind, k - 1],
            send_sem=rs_y.at[kind, k - 1], recv_sem=rr_y.at[kind, k - 1],
            device_id=(gx, lax.rem(gy + k, ny)), device_id_type=MESH)

    def reduce_start(kind, stage, value):
        red_src[kind, stage] = value
        for k in range(1, ny if stage else nx):
            reduce_copy(kind, stage, k).start()

    def reduce_wait(kind, stage):
        value = red_src[kind, stage]
        for k in range(1, ny if stage else nx):
            reduce_copy(kind, stage, k).wait_recv()
            value = value + (red_y if stage else red_x)[kind, k - 1]
        for k in range(1, ny if stage else nx):
            reduce_copy(kind, stage, k).wait_send()
        return value

    def face_copy(n, slot):
        d = DIRS[n]
        if n < 2:
            src = grad.at[:, pl.ds(cx if n == 0 else 0, 3)]
            dst = rx.at[slot, n]
        elif n < 4:
            src, dst = sy.at[n - 2], ry.at[slot, n - 2]
        else:
            src, dst = sc.at[n - 4], rc.at[slot, n - 4]
        return pltpu.make_async_remote_copy(
            src_ref=src, dst_ref=dst, send_sem=send_sem.at[slot, n], recv_sem=recv_sem.at[slot, n],
            device_id=(gx + d[0], gy + d[1]), device_id_type=MESH)

    sub = iota((8, nz), 0)

    def send_faces(slot):
        for n in range(2):
            @pl.when(can_send[n])
            def _():
                face_copy(n, slot).start()
        for side in range(2):
            tiles = []
            for c in range(comps):
                for k in range(3):
                    row = (high_rows, low_rows)[side][k]
                    tile = jnp.concatenate(
                        [grad[c, x, row : row + 1, :] for x in range(ex)]
                        + [jnp.zeros((8 - ex, nz), F32)], axis=0)
                    sy[side, 3 * c + k] = tile
                    tiles.append(tile)
            turned = [pltpu.roll(t, 4, 0) for t in tiles]
            for j in range(5):
                late = min(j + 5, 8)
                sc[2 * side, j] = jnp.where(sub < 4, turned[j], tiles[late])
                sc[2 * side + 1, j] = jnp.where(sub < 4, tiles[j], turned[late])
        for n in range(2, 8):
            @pl.when(can_send[n])
            def _():
                face_copy(n, slot).start()

    def recv_faces(slot):
        for n in range(8):
            @pl.when(can_recv[n])
            def _():
                face_copy(n, slot).wait_recv()
        for c in range(comps):
            for x in range(ex):
                value = grad[c, x]
                if x < 3:
                    value = value + rx[slot, 0, c, x]
                if x >= cx:
                    value = value + rx[slot, 1, c, x - cx]
                total[c, x] = value
        for side in range(2):
            for q in range(3 * comps):
                c, k = q // 3, q % 3
                row = (low_rows, high_rows)[side][k]
                below = rc[slot, 2 * side, q] if q < 5 else pltpu.roll(rc[slot, 2 * side, q - 5], 4, 0)
                above = pltpu.roll(rc[slot, 2 * side + 1, q], 4, 0) if q < 5 else rc[slot, 2 * side + 1, q - 5]
                tile = ry[slot, side, q] + jnp.where(sub < 3, below, jnp.where(sub > 3, above, 0.0))
                for x in range(ex):
                    total[c, x, row : row + 1, :] = total[c, x, row : row + 1, :] + tile[x : x + 1]

    def wait_sends(slot):
        for n in range(8):
            @pl.when(can_send[n])
            def _():
                face_copy(n, slot).wait_send()

    grad[...] = jnp.zeros_like(grad)
    grad[:, 1 : cx + 1, 0:cy, :] = coef_ref[...]
    mom[...] = jnp.zeros_like(mom)
    sec[...] = jnp.zeros_like(sec)
    for n in range(8):
        @pl.when(jnp.logical_not(can_recv[n]))
        def _():
            if n < 2:
                rx[:, n] = jnp.zeros((ITERS + 1, comps, 3, ey, nz), F32)
            elif n < 4:
                ry[:, n - 2] = jnp.zeros((ITERS + 1, 3 * comps, 8, nz), F32)
            else:
                rc[:, n - 4] = jnp.zeros((ITERS + 1, 5, 8, nz), F32)

    live = jnp.int32(0)
    for b in range(blocks):
        live = live + fill_ref[b]

    expected = jnp.int32(nx + ny - 2)
    for n in range(8):
        expected = expected + can_send[n].astype(jnp.int32)
    pl.semaphore_wait(barrier, expected)

    reduce_start(0, 0, jnp.full((8, nz), live, jnp.int32).astype(F32))
    send_faces(0)

    lane_b = iota((8, 16 * blocks), 1) // 16
    target = jnp.zeros((8, 16 * blocks), jnp.int32)
    ab_lane = iota((8, 16 * blocks), 1) % 16
    base_x = jnp.zeros((8, 16 * blocks), jnp.int32)
    base_y = jnp.zeros((8, 16 * blocks), jnp.int32)
    s_ab = iota((16, rows), 0)
    s_row = iota((16, rows), 1)
    zz = iota((nz, 128), 0)
    for b in range(blocks):
        cell = cell_ref[b]
        lx, ly, lz = cell // (cy * nz), cell // nz % cy, cell % nz
        base_x = jnp.where(lane_b == b, lx, base_x)
        base_y = jnp.where(lane_b == b, ly, base_y)
        y = ly - 1 + s_ab % 4
        y = jnp.where(y < 0, y + ey, y)
        sel_t[16 * b : 16 * (b + 1), :] = ((lx + s_ab // 4) * ey + y == s_row).astype(F32).astype(BF16)
        f = [frac_ref[c : c + 1, 128 * b : 128 * (b + 1)] for c in range(3)]
        bu, bv, bw = cubic(f[0]), cubic(f[1]), cubic(f[2])
        uv[b] = jnp.concatenate([bu[i] * bv[j] for i in range(4) for j in range(4)], axis=0)
        place = zz - (lz - 1)
        w = jnp.zeros((nz, 128), F32)
        for e in range(4):
            w = jnp.where(place == e, bw[e], w)
        wt_hi[b], wt_lo[b] = split(w)
    y = base_y - 1 + ab_lane % 4
    y = jnp.where(y < 0, y + ey, y)
    target = ((base_x + ab_lane // 4) * ey + y)[0:1]
    sel[...] = (iota((rows, 16 * blocks), 0) == target).astype(F32).astype(BF16)

    reduce_start(0, 1, reduce_wait(0, 0))
    recv_faces(0)
    cur[...] = total[...]
    wait_sends(0)
    grand = reduce_wait(0, 1)
    scale = (ncells / grand)[0:1]
    lane = iota((ey, nz), 1)
    y_row = iota((ey, nz), 0)
    own_y = y_row < cy
    top, bottom = gy == ny - 1, gy == 0
    mask_y = jnp.where(
        own_y, 1.0,
        jnp.where(y_row < cy + 2, jnp.where(top, 0.0, 1.0), jnp.where(bottom, 0.0, 1.0)),
    )
    mask_x = [None] * ex
    mask_x[0] = jnp.where(gx == 0, 0.0, 1.0)
    for x in range(cx + 1, ex):
        mask_x[x] = jnp.where(gx == nx - 1, 0.0, 1.0)

    def up_y(v):
        return pltpu.roll(v, ey - 1, 0)

    def down_y(v):
        return pltpu.roll(v, 1, 0)

    def up_z(v):
        return jnp.where(lane == nz - 1, 0.0, pltpu.roll(v, nz - 1, 1))

    def down_z(v):
        return jnp.where(lane == 0, 0.0, pltpu.roll(v, 1, 1))

    def forward(slot):
        parts = [split(cur[c].reshape(rows, nz)) for c in range(comps)]
        stack = jnp.concatenate([p[0] for p in parts] + [p[1] for p in parts], axis=1)
        picked = mm(sel_t[...], stack).astype(BF16)
        data = jnp.zeros((1, 128), F32)
        for b in range(blocks):
            r = slice(16 * b, 16 * (b + 1))
            hi = jnp.concatenate([picked[r, nz * c : nz * (c + 1)] for c in range(comps)], axis=0)
            lo = jnp.concatenate([picked[r, nz * (comps + c) : nz * (comps + c + 1)] for c in range(comps)], axis=0)
            whi, wlo = wt_hi[b], wt_lo[b]
            q = mm(hi, whi) + mm(lo, whi) + mm(hi, wlo)
            u = uv[b]
            alive = iota((1, 128), 1) < fill_ref[b]
            back = []
            for c in range(comps):
                v = jnp.sum(q[16 * c : 16 * (c + 1)] * u, axis=0, keepdims=True)
                mis = jnp.where(alive, v - targ_ref[c : c + 1, 128 * b : 128 * (b + 1)], 0.0)
                data = data + mis * mis
                back.append((mis * (2.0 * scale)) * u)
            dhi, dlo = split(jnp.concatenate(back, axis=0))
            t = mm_nt(dhi, whi) + mm_nt(dlo, whi) + mm_nt(dhi, wlo)
            thi, tlo = split(t)
            for c in range(comps):
                term[r, nz * c : nz * (c + 1)] = thi[16 * c : 16 * (c + 1)]
                term[r, nz * (comps + c) : nz * (comps + c + 1)] = tlo[16 * c : 16 * (c + 1)]
        pulled = mm(sel[...], term[...])
        spread = jnp.zeros((ey, nz), F32)
        div = []
        for x in range(1, cx + 1):
            one, two = cur[1, x], cur[2, x]
            dv = (cur[0, x + 1] - cur[0, x - 1] + up_y(one) - down_y(one) + up_z(two) - down_z(two)) / 2.0
            dv = jnp.where(own_y, dv, 0.0)
            spread = spread + dv * dv
            div.append(dv)
        for c in range(comps):
            whole = pulled[:, nz * c : nz * (c + 1)] + pulled[:, nz * (comps + c) : nz * (comps + c + 1)]
            for x in range(ex):
                value = whole[ey * x : ey * (x + 1)]
                if c == 0:
                    if 0 <= x - 2 < cx:
                        value = value + penalty_weight * div[x - 2]
                    if x < cx:
                        value = value - penalty_weight * div[x]
                elif 1 <= x <= cx:
                    dv = div[x - 1]
                    if c == 1:
                        value = value + penalty_weight * (down_y(dv) - up_y(dv))
                    else:
                        value = value + penalty_weight * (down_z(dv) - up_z(dv))
                grad[c, x] = value
        return data * (scale / ncells) + (penalty_weight / ncells) * jnp.sum(spread, axis=0, keepdims=True)

    def update(step):
        def pick(values):
            out = jnp.float32(values[-1])
            for i in range(ITERS - 1):
                out = jnp.where(step == i, jnp.float32(values[i]), out)
            return out
        rate = pick([learn_rate / (1.0 - beta_one ** (i + 1)) for i in range(ITERS)])
        corr = pick([1.0 / (1.0 - beta_two ** (i + 1)) for i in range(ITERS)])
        for c in range(comps):
            for x in range(ex):
                g = total[c, x] * mask_y
                if mask_x[x] is not None:
                    g = g * mask_x[x]
                m = beta_one * mom[c, x] + (1.0 - beta_one) * g
                s = beta_two * sec[c, x] + (1.0 - beta_two) * g * g
                mom[c, x], sec[c, x] = m, s
                cur[c, x] = cur[c, x] - (rate * m) / (jnp.sqrt(s * corr) + adam_eps)

    def body(step, losses):
        loss = forward(step)
        losses = jnp.where(sub == step, loss, losses)
        send_faces(step + 1)

        @pl.when(step == ITERS - 1)
        def _():
            reduce_start(1, 0, losses)

        recv_faces(step + 1)

        @pl.when(step == ITERS - 1)
        def _():
            reduce_start(1, 1, reduce_wait(1, 0))

        update(step)
        wait_sends(step + 1)
        return losses

    lax.fori_loop(0, ITERS, body, jnp.zeros((8, nz), F32))
    out_ref[...] = cur[:, 1 : cx + 1, 0:cy, :]
    final = reduce_wait(1, 1)
    for i in range(ITERS):
        loss_ref[i] = jnp.sum(final[i : i + 1])


def shards(nx, ny, coefficients, fractions, targets, block_cell, block_fill):
    comps, cx, cy, nz = coefficients.shape
    blocks = block_cell.shape[0]
    ex, ey = cx + 3, cy + 8
    rows = ex * ey
    state = pltpu.VMEM((comps, ex, ey, nz), F32)
    smem = pl.BlockSpec(memory_space=pltpu.SMEM)
    vmem = pl.BlockSpec(memory_space=pltpu.VMEM)
    dma = pltpu.SemaphoreType.DMA
    slots = ITERS + 1
    return pl.pallas_call(
        functools.partial(kernel, nx, ny),
        out_shape=(
            jax.ShapeDtypeStruct(coefficients.shape, F32),
            jax.ShapeDtypeStruct((ITERS,), F32),
        ),
        in_specs=[smem, smem, vmem, vmem, vmem],
        out_specs=(vmem, smem),
        scratch_shapes=[
            state, state, state, state, state,
            pltpu.VMEM((blocks, nz, 128), BF16),
            pltpu.VMEM((blocks, nz, 128), BF16),
            pltpu.VMEM((blocks, 16, 128), F32),
            pltpu.VMEM((rows, 16 * blocks), BF16),
            pltpu.VMEM((16 * blocks, rows), BF16),
            pltpu.VMEM((16 * blocks, 2 * comps * nz), BF16),
            pltpu.VMEM((2, 3 * comps, 8, nz), F32),
            pltpu.VMEM((4, 5, 8, nz), F32),
            pltpu.VMEM((slots, 2, comps, 3, ey, nz), F32),
            pltpu.VMEM((slots, 2, 3 * comps, 8, nz), F32),
            pltpu.VMEM((slots, 4, 5, 8, nz), F32),
            pltpu.VMEM((2, 2, 8, nz), F32),
            pltpu.VMEM((2, nx - 1, 8, nz), F32),
            pltpu.VMEM((2, ny - 1, 8, nz), F32),
            dma((slots, 8)), dma((slots, 8)),
            dma((2, nx - 1)), dma((2, nx - 1)),
            dma((2, ny - 1)), dma((2, ny - 1)),
        ],
        compiler_params=pltpu.CompilerParams(
            collective_id=0, has_side_effects=True, vmem_limit_bytes=32 * 1024 * 1024
        ),
    )(block_cell, block_fill, coefficients, fractions, targets)


def solution(mesh):
    nx, ny = mesh.shape["gx"], mesh.shape["gy"]
    return jax.shard_map(
        functools.partial(shards, nx, ny),
        mesh=mesh,
        in_specs=(
            P(None, "gx", "gy", None),
            P(None, ("gx", "gy")),
            P(None, ("gx", "gy")),
            P(("gx", "gy")),
            P(("gx", "gy")),
        ),
        out_specs=(P(None, "gx", "gy", None), P()),
        check_vma=False,
    )
```

```python
import functools

import jax
import jax.numpy as jnp
from jax import lax
from jax.experimental import pallas as pl
from jax.experimental.pallas import tpu as pltpu
from jax.sharding import PartitionSpec as P

ITERS = 4

penalty_weight = 0.5
learn_rate = 0.05
beta_one = 0.9
beta_two = 0.999
adam_eps = 0.1

MESH = pl.DeviceIdType.MESH
DIRS = ((1, 0), (-1, 0), (0, 1), (0, -1), (1, 1), (-1, 1), (1, -1), (-1, -1))
F32 = jnp.float32
BF16 = jnp.bfloat16


def cubic(u):
    one = 1.0 - u
    return (
        one * one * one / 6.0,
        (3.0 * u * u * u - 6.0 * u * u + 4.0) / 6.0,
        (-3.0 * u * u * u + 3.0 * u * u + 3.0 * u + 1.0) / 6.0,
        u * u * u / 6.0,
    )


def split(x):
    hi = x.astype(BF16)
    lo = (x - hi.astype(F32)).astype(BF16)
    return hi, lo


def mm(a, b):
    return jnp.dot(a, b, preferred_element_type=F32)


def folded(hi, lo, w):
    both = mm(jnp.concatenate([hi, lo], axis=1), w)
    half = both.shape[1] // 2
    return both[:, :half] + both[:, half:]


def iota(shape, dim):
    return lax.broadcasted_iota(jnp.int32, shape, dim)


def kernel(
    nx, ny, cell_in, fill_in, coef_in, frac_in, targ_in, out_ref, loss_ref,
    cell_ref, fill_ref, coef_ref, frac_ref, targ_ref, in_sem,
    cur, mom, sec, grad, total, w_ahead, w_back, uv, sel, sel_t, term, sy, sc, rx, ry, rc,
    red_src, red_x, red_y, send_sem, recv_sem, rs_x, rr_x, rs_y, rr_y,
):
    loads = [
        pltpu.make_async_copy(src, dst, in_sem.at[n])
        for n, (src, dst) in enumerate((
            (coef_in, coef_ref), (fill_in, fill_ref), (cell_in, cell_ref),
            (frac_in, frac_ref), (targ_in, targ_ref)))
    ]
    for load in loads:
        load.start()
    comps, cx, cy, nz = coef_ref.shape
    blocks = cell_ref.shape[0]
    ex, ey = cx + 3, cy + 8
    rows = ex * ey
    gx, gy = lax.axis_index("gx"), lax.axis_index("gy")
    ncells = float(cx * nx * cy * ny * nz)
    low_rows = (ey - 1, 0, 1)
    high_rows = (cy - 1, cy, cy + 1)

    def here(d, sign):
        x, y = gx + sign * d[0], gy + sign * d[1]
        return (x >= 0) & (x < nx) & (y >= 0) & (y < ny)

    can_send = [here(d, 1) for d in DIRS]
    can_recv = [here(d, -1) for d in DIRS]

    barrier = pltpu.get_barrier_semaphore()
    for n, d in enumerate(DIRS):
        @pl.when(can_send[n])
        def _():
            pl.semaphore_signal(barrier, inc=1, device_id=(gx + d[0], gy + d[1]), device_id_type=MESH)
    for k in range(1, nx):
        pl.semaphore_signal(barrier, inc=1, device_id=(lax.rem(gx + k, nx), gy), device_id_type=MESH)
    for k in range(1, ny):
        pl.semaphore_signal(barrier, inc=1, device_id=(gx, lax.rem(gy + k, ny)), device_id_type=MESH)

    def reduce_copy(kind, stage, k):
        if stage == 0:
            return pltpu.make_async_remote_copy(
                src_ref=red_src.at[kind, 0], dst_ref=red_x.at[kind, k - 1],
                send_sem=rs_x.at[kind, k - 1], recv_sem=rr_x.at[kind, k - 1],
                device_id=(lax.rem(gx + k, nx), gy), device_id_type=MESH)
        return pltpu.make_async_remote_copy(
            src_ref=red_src.at[kind, 1], dst_ref=red_y.at[kind, k - 1],
            send_sem=rs_y.at[kind, k - 1], recv_sem=rr_y.at[kind, k - 1],
            device_id=(gx, lax.rem(gy + k, ny)), device_id_type=MESH)

    def reduce_start(kind, stage, value):
        red_src[kind, stage] = value
        for k in range(1, ny if stage else nx):
            reduce_copy(kind, stage, k).start()

    def reduce_wait(kind, stage):
        value = red_src[kind, stage]
        for k in range(1, ny if stage else nx):
            reduce_copy(kind, stage, k).wait_recv()
            value = value + (red_y if stage else red_x)[kind, k - 1]
        for k in range(1, ny if stage else nx):
            reduce_copy(kind, stage, k).wait_send()
        return value

    def face_copy(n, slot):
        d = DIRS[n]
        if n < 2:
            src = grad.at[:, pl.ds(cx if n == 0 else 0, 3)]
            dst = rx.at[slot, n]
        elif n < 4:
            src, dst = sy.at[n - 2], ry.at[slot, n - 2]
        else:
            src, dst = sc.at[n - 4], rc.at[slot, n - 4]
        return pltpu.make_async_remote_copy(
            src_ref=src, dst_ref=dst, send_sem=send_sem.at[slot, n], recv_sem=recv_sem.at[slot, n],
            device_id=(gx + d[0], gy + d[1]), device_id_type=MESH)

    sub = iota((8, nz), 0)

    def send_faces(slot):
        for n in range(2):
            @pl.when(can_send[n])
            def _():
                face_copy(n, slot).start()
        for side in range(2):
            tiles = []
            for c in range(comps):
                for k in range(3):
                    row = (high_rows, low_rows)[side][k]
                    tile = jnp.concatenate(
                        [grad[c, x, row : row + 1, :] for x in range(ex)]
                        + [jnp.zeros((8 - ex, nz), F32)], axis=0)
                    sy[side, 3 * c + k] = tile
                    tiles.append(tile)
            turned = [pltpu.roll(t, 4, 0) for t in tiles]
            for j in range(5):
                late = min(j + 5, 8)
                sc[2 * side, j] = jnp.where(sub < 4, turned[j], tiles[late])
                sc[2 * side + 1, j] = jnp.where(sub < 4, tiles[j], turned[late])
        for n in range(2, 8):
            @pl.when(can_send[n])
            def _():
                face_copy(n, slot).start()

    def recv_faces(slot):
        for n in range(8):
            @pl.when(can_recv[n])
            def _():
                face_copy(n, slot).wait_recv()
        for c in range(comps):
            for x in range(ex):
                value = grad[c, x]
                if x < 3:
                    value = value + rx[slot, 0, c, x]
                if x >= cx:
                    value = value + rx[slot, 1, c, x - cx]
                total[c, x] = value
        for side in range(2):
            for q in range(3 * comps):
                c, k = q // 3, q % 3
                row = (low_rows, high_rows)[side][k]
                below = rc[slot, 2 * side, q] if q < 5 else pltpu.roll(rc[slot, 2 * side, q - 5], 4, 0)
                above = pltpu.roll(rc[slot, 2 * side + 1, q], 4, 0) if q < 5 else rc[slot, 2 * side + 1, q - 5]
                tile = ry[slot, side, q] + jnp.where(sub < 3, below, jnp.where(sub > 3, above, 0.0))
                for x in range(ex):
                    total[c, x, row : row + 1, :] = total[c, x, row : row + 1, :] + tile[x : x + 1]

    def wait_sends(slot):
        for n in range(8):
            @pl.when(can_send[n])
            def _():
                face_copy(n, slot).wait_send()

    grad[...] = jnp.zeros_like(grad)
    mom[...] = jnp.zeros_like(mom)
    sec[...] = jnp.zeros_like(sec)
    for n in range(8):
        @pl.when(jnp.logical_not(can_recv[n]))
        def _():
            if n < 2:
                rx[:, n] = jnp.zeros((ITERS + 1, comps, 3, ey, nz), F32)
            elif n < 4:
                ry[:, n - 2] = jnp.zeros((ITERS + 1, 3 * comps, 8, nz), F32)
            else:
                rc[:, n - 4] = jnp.zeros((ITERS + 1, 5, 8, nz), F32)

    for load in loads:
        load.wait()
    grad[:, 1 : cx + 1, 0:cy, :] = coef_ref[...]
    live = jnp.int32(0)
    for b in range(blocks):
        live = live + fill_ref[b]

    expected = jnp.int32(nx + ny - 2)
    for n in range(8):
        expected = expected + can_send[n].astype(jnp.int32)
    pl.semaphore_wait(barrier, expected)

    reduce_start(0, 0, jnp.full((8, nz), live, jnp.int32).astype(F32))
    send_faces(0)

    lane_b = iota((8, 16 * blocks), 1) // 16
    target = jnp.zeros((8, 16 * blocks), jnp.int32)
    ab_lane = iota((8, 16 * blocks), 1) % 16
    base_x = jnp.zeros((8, 16 * blocks), jnp.int32)
    base_y = jnp.zeros((8, 16 * blocks), jnp.int32)
    s_ab = iota((16, rows), 0)
    s_row = iota((16, rows), 1)
    zz = iota((nz, 128), 0)
    for b in range(blocks):
        cell = cell_ref[b]
        lx, ly, lz = cell // (cy * nz), cell // nz % cy, cell % nz
        base_x = jnp.where(lane_b == b, lx, base_x)
        base_y = jnp.where(lane_b == b, ly, base_y)
        y = ly - 1 + s_ab % 4
        y = jnp.where(y < 0, y + ey, y)
        sel_t[16 * b : 16 * (b + 1), :] = ((lx + s_ab // 4) * ey + y == s_row).astype(F32).astype(BF16)
        f = [frac_ref[c : c + 1, 128 * b : 128 * (b + 1)] for c in range(3)]
        bu, bv, bw = cubic(f[0]), cubic(f[1]), cubic(f[2])
        uv[b] = jnp.concatenate([bu[i] * bv[j] for i in range(4) for j in range(4)], axis=0)
        place = zz - (lz - 1)
        w = jnp.zeros((nz, 128), F32)
        for e in range(4):
            w = jnp.where(place == e, bw[e], w)
        for mat, ref in ((w, w_ahead), (w.T, w_back)):
            hi, lo = split(mat)
            ref[b] = jnp.concatenate(
                [jnp.concatenate([hi, lo], axis=1), jnp.concatenate([hi, jnp.zeros_like(lo)], axis=1)], axis=0)
    y = base_y - 1 + ab_lane % 4
    y = jnp.where(y < 0, y + ey, y)
    target = ((base_x + ab_lane // 4) * ey + y)[0:1]
    sel[...] = (iota((rows, 16 * blocks), 0) == target).astype(F32).astype(BF16)

    reduce_start(0, 1, reduce_wait(0, 0))
    recv_faces(0)
    cur[...] = total[...]
    wait_sends(0)
    lane = iota((ey, nz), 1)
    y_row = iota((ey, nz), 0)
    own_y = y_row < cy
    top, bottom = gy == ny - 1, gy == 0
    mask_y = jnp.where(
        own_y, 1.0,
        jnp.where(y_row < cy + 2, jnp.where(top, 0.0, 1.0), jnp.where(bottom, 0.0, 1.0)),
    )
    mask_x = [None] * ex
    mask_x[0] = jnp.where(gx == 0, 0.0, 1.0)
    for x in range(cx + 1, ex):
        mask_x[x] = jnp.where(gx == nx - 1, 0.0, 1.0)

    def up_y(v):
        return pltpu.roll(v, ey - 1, 0)

    def down_y(v):
        return pltpu.roll(v, 1, 0)

    def up_z(v):
        return jnp.where(lane == nz - 1, 0.0, pltpu.roll(v, nz - 1, 1))

    def down_z(v):
        return jnp.where(lane == 0, 0.0, pltpu.roll(v, 1, 1))

    def scale():
        value = red_src[0, 1]
        for k in range(1, ny):
            value = value + red_y[0, k - 1]
        return (ncells / value)[0:1]

    def forward(step):
        parts = [split(cur[c].reshape(rows, nz)) for c in range(comps)]
        stack = jnp.concatenate([p[0] for p in parts] + [p[1] for p in parts], axis=1)
        picked = mm(sel_t[...], stack).astype(BF16)
        data = jnp.zeros((1, 128), F32)
        for b in range(blocks):
            r = slice(16 * b, 16 * (b + 1))
            hi = jnp.concatenate([picked[r, nz * c : nz * (c + 1)] for c in range(comps)], axis=0)
            lo = jnp.concatenate([picked[r, nz * (comps + c) : nz * (comps + c + 1)] for c in range(comps)], axis=0)
            q = folded(hi, lo, w_ahead[b])
            u = uv[b]
            alive = iota((1, 128), 1) < fill_ref[b]
            back = []
            for c in range(comps):
                v = jnp.sum(q[16 * c : 16 * (c + 1)] * u, axis=0, keepdims=True)
                mis = jnp.where(alive, v - targ_ref[c : c + 1, 128 * b : 128 * (b + 1)], 0.0)
                data = data + mis * mis
                back.append((mis * 2.0) * u)
            dhi, dlo = split(jnp.concatenate(back, axis=0))
            t = folded(dhi, dlo, w_back[b])
            thi, tlo = split(t)
            for c in range(comps):
                term[r, nz * c : nz * (c + 1)] = thi[16 * c : 16 * (c + 1)]
                term[r, nz * (comps + c) : nz * (comps + c + 1)] = tlo[16 * c : 16 * (c + 1)]
        pulled = mm(sel[...], term[...])

        @pl.when(step == 0)
        def _():
            reduce_wait(0, 1)

        ratio = scale()
        spread = jnp.zeros((ey, nz), F32)
        div = []
        for x in range(1, cx + 1):
            one, two = cur[1, x], cur[2, x]
            dv = (cur[0, x + 1] - cur[0, x - 1] + up_y(one) - down_y(one) + up_z(two) - down_z(two)) / 2.0
            dv = jnp.where(own_y, dv, 0.0)
            spread = spread + dv * dv
            div.append(dv)
        for c in range(comps):
            whole = ratio * (pulled[:, nz * c : nz * (c + 1)] + pulled[:, nz * (comps + c) : nz * (comps + c + 1)])
            for x in range(ex):
                value = whole[ey * x : ey * (x + 1)]
                if c == 0:
                    if 0 <= x - 2 < cx:
                        value = value + penalty_weight * div[x - 2]
                    if x < cx:
                        value = value - penalty_weight * div[x]
                elif 1 <= x <= cx:
                    dv = div[x - 1]
                    if c == 1:
                        value = value + penalty_weight * (down_y(dv) - up_y(dv))
                    else:
                        value = value + penalty_weight * (down_z(dv) - up_z(dv))
                grad[c, x] = value
        return data * (ratio / ncells) + (penalty_weight / ncells) * jnp.sum(spread, axis=0, keepdims=True)

    def update(step):
        def pick(values):
            out = jnp.float32(values[-1])
            for i in range(ITERS - 1):
                out = jnp.where(step == i, jnp.float32(values[i]), out)
            return out
        rate = pick([learn_rate / (1.0 - beta_one ** (i + 1)) for i in range(ITERS)])
        corr = pick([1.0 / (1.0 - beta_two ** (i + 1)) for i in range(ITERS)])
        for c in range(comps):
            for x in range(ex):
                g = total[c, x] * mask_y
                if mask_x[x] is not None:
                    g = g * mask_x[x]
                m = beta_one * mom[c, x] + (1.0 - beta_one) * g
                s = beta_two * sec[c, x] + (1.0 - beta_two) * g * g
                mom[c, x], sec[c, x] = m, s
                cur[c, x] = cur[c, x] - (rate * m) / (jnp.sqrt(s * corr) + adam_eps)

    def body(step, losses):
        loss = forward(step)
        losses = jnp.where(sub == step, loss, losses)

        @pl.when(step == ITERS - 1)
        def _():
            reduce_start(1, 0, losses)

        send_faces(step + 1)

        @pl.when(step == ITERS - 1)
        def _():
            reduce_start(1, 1, reduce_wait(1, 0))

        recv_faces(step + 1)

        update(step)
        wait_sends(step + 1)
        return losses

    lax.fori_loop(0, ITERS, body, jnp.zeros((8, nz), F32))
    out_ref[...] = cur[:, 1 : cx + 1, 0:cy, :]
    final = reduce_wait(1, 1)
    for i in range(ITERS):
        loss_ref[i] = jnp.sum(final[i : i + 1])


def shards(nx, ny, coefficients, fractions, targets, block_cell, block_fill):
    comps, cx, cy, nz = coefficients.shape
    blocks = block_cell.shape[0]
    ex, ey = cx + 3, cy + 8
    rows = ex * ey
    state = pltpu.VMEM((comps, ex, ey, nz), F32)
    smem = pl.BlockSpec(memory_space=pltpu.SMEM)
    vmem = pl.BlockSpec(memory_space=pltpu.VMEM)
    dma = pltpu.SemaphoreType.DMA
    slots = ITERS + 1
    return pl.pallas_call(
        functools.partial(kernel, nx, ny),
        out_shape=(
            jax.ShapeDtypeStruct(coefficients.shape, F32),
            jax.ShapeDtypeStruct((ITERS,), F32),
        ),
        in_specs=[pl.BlockSpec(memory_space=pltpu.HBM)] * 5,
        out_specs=(vmem, smem),
        scratch_shapes=[
            pltpu.SMEM((blocks,), jnp.int32),
            pltpu.SMEM((blocks,), jnp.int32),
            pltpu.VMEM(coefficients.shape, F32),
            pltpu.VMEM(fractions.shape, F32),
            pltpu.VMEM(targets.shape, F32),
            dma((5,)),
            state, state, state, state, state,
            pltpu.VMEM((blocks, 2 * nz, 256), BF16),
            pltpu.VMEM((blocks, 256, 2 * nz), BF16),
            pltpu.VMEM((blocks, 16, 128), F32),
            pltpu.VMEM((rows, 16 * blocks), BF16),
            pltpu.VMEM((16 * blocks, rows), BF16),
            pltpu.VMEM((16 * blocks, 2 * comps * nz), BF16),
            pltpu.VMEM((2, 3 * comps, 8, nz), F32),
            pltpu.VMEM((4, 5, 8, nz), F32),
            pltpu.VMEM((slots, 2, comps, 3, ey, nz), F32),
            pltpu.VMEM((slots, 2, 3 * comps, 8, nz), F32),
            pltpu.VMEM((slots, 4, 5, 8, nz), F32),
            pltpu.VMEM((2, 2, 8, nz), F32),
            pltpu.VMEM((2, nx - 1, 8, nz), F32),
            pltpu.VMEM((2, ny - 1, 8, nz), F32),
            dma((slots, 8)), dma((slots, 8)),
            dma((2, nx - 1)), dma((2, nx - 1)),
            dma((2, ny - 1)), dma((2, ny - 1)),
        ],
        compiler_params=pltpu.CompilerParams(
            collective_id=0, has_side_effects=True, vmem_limit_bytes=60 * 1024 * 1024
        ),
    )(block_cell, block_fill, coefficients, fractions, targets)


def solution(mesh):
    nx, ny = mesh.shape["gx"], mesh.shape["gy"]
    return jax.shard_map(
        functools.partial(shards, nx, ny),
        mesh=mesh,
        in_specs=(
            P(None, "gx", "gy", None),
            P(None, ("gx", "gy")),
            P(None, ("gx", "gy")),
            P(("gx", "gy")),
            P(("gx", "gy")),
        ),
        out_specs=(P(None, "gx", "gy", None), P()),
        check_vma=False,
    )
```

```python
import functools

import jax
import jax.numpy as jnp
from jax import lax
from jax.experimental import pallas as pl
from jax.experimental.pallas import tpu as pltpu
from jax.sharding import PartitionSpec as P

ITERS = 4

penalty_weight = 0.5
learn_rate = 0.05
beta_one = 0.9
beta_two = 0.999
adam_eps = 0.1

MESH = pl.DeviceIdType.MESH
DIRS = ((1, 0), (-1, 0), (0, 1), (0, -1), (1, 1), (-1, 1), (1, -1), (-1, -1))
F32 = jnp.float32
BF16 = jnp.bfloat16


def cubic(u):
    one = 1.0 - u
    return (
        one * one * one / 6.0,
        (3.0 * u * u * u - 6.0 * u * u + 4.0) / 6.0,
        (-3.0 * u * u * u + 3.0 * u * u + 3.0 * u + 1.0) / 6.0,
        u * u * u / 6.0,
    )


def split(x):
    hi = x.astype(BF16)
    lo = (x - hi.astype(F32)).astype(BF16)
    return hi, lo


def mm(a, b):
    return jnp.dot(a, b, preferred_element_type=F32)


def folded(hi, lo, w):
    both = mm(jnp.concatenate([hi, lo], axis=1), w)
    half = both.shape[1] // 2
    return both[:, :half] + both[:, half:]


def iota(shape, dim):
    return lax.broadcasted_iota(jnp.int32, shape, dim)


def kernel(
    nx, ny, cell_in, fill_in, coef_in, frac_in, targ_in, out_ref, loss_ref,
    cell_ref, fill_ref, coef_ref, frac_ref, targ_ref, in_sem,
    cur, mom, sec, grad, total, w_ahead, w_back, uv, sel, sel_t, term, sy, sc, rx, ry, rc,
    red_src, red_x, red_y, send_sem, recv_sem, rs_x, rr_x, rs_y, rr_y,
):
    loads = [
        pltpu.make_async_copy(src, dst, in_sem.at[n])
        for n, (src, dst) in enumerate((
            (coef_in, coef_ref), (fill_in, fill_ref), (cell_in, cell_ref),
            (frac_in, frac_ref), (targ_in, targ_ref)))
    ]
    for load in loads:
        load.start()
    comps, cx, cy, nz = coef_ref.shape
    blocks = cell_ref.shape[0]
    ex, ey = cx + 3, cy + 8
    rows = ex * ey
    gx, gy = lax.axis_index("gx"), lax.axis_index("gy")
    ncells = float(cx * nx * cy * ny * nz)
    low_rows = (ey - 1, 0, 1)
    high_rows = (cy - 1, cy, cy + 1)

    def here(d, sign):
        x, y = gx + sign * d[0], gy + sign * d[1]
        return (x >= 0) & (x < nx) & (y >= 0) & (y < ny)

    can_send = [here(d, 1) for d in DIRS]
    can_recv = [here(d, -1) for d in DIRS]

    barrier = pltpu.get_barrier_semaphore()
    for n, d in enumerate(DIRS):
        @pl.when(can_send[n])
        def _():
            pl.semaphore_signal(barrier, inc=1, device_id=(gx + d[0], gy + d[1]), device_id_type=MESH)
    for k in range(1, nx):
        pl.semaphore_signal(barrier, inc=1, device_id=(lax.rem(gx + k, nx), gy), device_id_type=MESH)
    for k in range(1, ny):
        pl.semaphore_signal(barrier, inc=1, device_id=(gx, lax.rem(gy + k, ny)), device_id_type=MESH)

    def reduce_copy(kind, stage, k):
        if stage == 0:
            return pltpu.make_async_remote_copy(
                src_ref=red_src.at[kind, 0], dst_ref=red_x.at[kind, k - 1],
                send_sem=rs_x.at[kind, k - 1], recv_sem=rr_x.at[kind, k - 1],
                device_id=(lax.rem(gx + k, nx), gy), device_id_type=MESH)
        return pltpu.make_async_remote_copy(
            src_ref=red_src.at[kind, 1], dst_ref=red_y.at[kind, k - 1],
            send_sem=rs_y.at[kind, k - 1], recv_sem=rr_y.at[kind, k - 1],
            device_id=(gx, lax.rem(gy + k, ny)), device_id_type=MESH)

    def reduce_start(kind, stage, value):
        red_src[kind, stage] = value
        for k in range(1, ny if stage else nx):
            reduce_copy(kind, stage, k).start()

    def reduce_wait(kind, stage):
        value = red_src[kind, stage]
        for k in range(1, ny if stage else nx):
            reduce_copy(kind, stage, k).wait_recv()
            value = value + (red_y if stage else red_x)[kind, k - 1]
        for k in range(1, ny if stage else nx):
            reduce_copy(kind, stage, k).wait_send()
        return value

    def face_copy(n, slot):
        d = DIRS[n]
        if n < 2:
            src = grad.at[:, pl.ds(cx if n == 0 else 0, 3)]
            dst = rx.at[slot, n]
        elif n < 4:
            src, dst = sy.at[n - 2], ry.at[slot, n - 2]
        else:
            src, dst = sc.at[n - 4], rc.at[slot, n - 4]
        return pltpu.make_async_remote_copy(
            src_ref=src, dst_ref=dst, send_sem=send_sem.at[slot, n], recv_sem=recv_sem.at[slot, n],
            device_id=(gx + d[0], gy + d[1]), device_id_type=MESH)

    sub = iota((8, nz), 0)

    def send_faces(slot):
        for side in range(2):
            tiles = []
            for c in range(comps):
                for k in range(3):
                    row = (high_rows, low_rows)[side][k]
                    tile = jnp.concatenate(
                        [grad[c, x, row : row + 1, :] for x in range(ex)]
                        + [jnp.zeros((8 - ex, nz), F32)], axis=0)
                    sy[side, 3 * c + k] = tile
                    tiles.append(tile)
            turned = [pltpu.roll(t, 4, 0) for t in tiles]
            for j in range(5):
                late = min(j + 5, 8)
                sc[2 * side, j] = jnp.where(sub < 4, turned[j], tiles[late])
                sc[2 * side + 1, j] = jnp.where(sub < 4, tiles[j], turned[late])
        for n in (4, 5, 6, 7, 2, 3, 0, 1):
            @pl.when(can_send[n])
            def _():
                face_copy(n, slot).start()

    def recv_faces(slot):
        for n in range(8):
            @pl.when(can_recv[n])
            def _():
                face_copy(n, slot).wait_recv()
        for c in range(comps):
            for x in range(ex):
                value = grad[c, x]
                if x < 3:
                    value = value + rx[slot, 0, c, x]
                if x >= cx:
                    value = value + rx[slot, 1, c, x - cx]
                total[c, x] = value
        for side in range(2):
            for q in range(3 * comps):
                c, k = q // 3, q % 3
                row = (low_rows, high_rows)[side][k]
                below = rc[slot, 2 * side, q] if q < 5 else pltpu.roll(rc[slot, 2 * side, q - 5], 4, 0)
                above = pltpu.roll(rc[slot, 2 * side + 1, q], 4, 0) if q < 5 else rc[slot, 2 * side + 1, q - 5]
                tile = ry[slot, side, q] + jnp.where(sub < 3, below, jnp.where(sub > 3, above, 0.0))
                for x in range(ex):
                    total[c, x, row : row + 1, :] = total[c, x, row : row + 1, :] + tile[x : x + 1]

    def wait_sends(slot):
        for n in range(8):
            @pl.when(can_send[n])
            def _():
                face_copy(n, slot).wait_send()

    grad[...] = jnp.zeros_like(grad)
    mom[...] = jnp.zeros_like(mom)
    sec[...] = jnp.zeros_like(sec)
    for n in range(8):
        @pl.when(jnp.logical_not(can_recv[n]))
        def _():
            if n < 2:
                rx[:, n] = jnp.zeros((ITERS + 1, comps, 3, ey, nz), F32)
            elif n < 4:
                ry[:, n - 2] = jnp.zeros((ITERS + 1, 3 * comps, 8, nz), F32)
            else:
                rc[:, n - 4] = jnp.zeros((ITERS + 1, 5, 8, nz), F32)

    for load in loads:
        load.wait()
    grad[:, 1 : cx + 1, 0:cy, :] = coef_ref[...]
    live = jnp.int32(0)
    for b in range(blocks):
        live = live + fill_ref[b]

    expected = jnp.int32(nx + ny - 2)
    for n in range(8):
        expected = expected + can_send[n].astype(jnp.int32)
    pl.semaphore_wait(barrier, expected)

    reduce_start(0, 0, jnp.full((8, nz), live, jnp.int32).astype(F32))
    send_faces(0)

    lane_b = iota((8, 16 * blocks), 1) // 16
    target = jnp.zeros((8, 16 * blocks), jnp.int32)
    ab_lane = iota((8, 16 * blocks), 1) % 16
    base_x = jnp.zeros((8, 16 * blocks), jnp.int32)
    base_y = jnp.zeros((8, 16 * blocks), jnp.int32)
    s_ab = iota((16, rows), 0)
    s_row = iota((16, rows), 1)
    zz = iota((nz, 128), 0)
    for b in range(blocks):
        cell = cell_ref[b]
        lx, ly, lz = cell // (cy * nz), cell // nz % cy, cell % nz
        base_x = jnp.where(lane_b == b, lx, base_x)
        base_y = jnp.where(lane_b == b, ly, base_y)
        y = ly - 1 + s_ab % 4
        y = jnp.where(y < 0, y + ey, y)
        sel_t[16 * b : 16 * (b + 1), :] = ((lx + s_ab // 4) * ey + y == s_row).astype(F32).astype(BF16)
        f = [frac_ref[c : c + 1, 128 * b : 128 * (b + 1)] for c in range(3)]
        bu, bv, bw = cubic(f[0]), cubic(f[1]), cubic(f[2])
        uv[b] = jnp.concatenate([bu[i] * bv[j] for i in range(4) for j in range(4)], axis=0)
        place = zz - (lz - 1)
        w = jnp.zeros((nz, 128), F32)
        for e in range(4):
            w = jnp.where(place == e, bw[e], w)
        for mat, ref in ((w, w_ahead), (w.T, w_back)):
            hi, lo = split(mat)
            ref[b] = jnp.concatenate(
                [jnp.concatenate([hi, lo], axis=1), jnp.concatenate([hi, jnp.zeros_like(lo)], axis=1)], axis=0)
    y = base_y - 1 + ab_lane % 4
    y = jnp.where(y < 0, y + ey, y)
    target = ((base_x + ab_lane // 4) * ey + y)[0:1]
    sel[...] = (iota((rows, 16 * blocks), 0) == target).astype(F32).astype(BF16)

    reduce_start(0, 1, reduce_wait(0, 0))
    recv_faces(0)
    cur[...] = total[...]
    wait_sends(0)
    lane = iota((ey, nz), 1)
    y_row = iota((ey, nz), 0)
    own_y = y_row < cy
    top, bottom = gy == ny - 1, gy == 0
    mask_y = jnp.where(
        own_y, 1.0,
        jnp.where(y_row < cy + 2, jnp.where(top, 0.0, 1.0), jnp.where(bottom, 0.0, 1.0)),
    )
    mask_x = [None] * ex
    mask_x[0] = jnp.where(gx == 0, 0.0, 1.0)
    for x in range(cx + 1, ex):
        mask_x[x] = jnp.where(gx == nx - 1, 0.0, 1.0)

    def up_y(v):
        return pltpu.roll(v, ey - 1, 0)

    def down_y(v):
        return pltpu.roll(v, 1, 0)

    def up_z(v):
        return jnp.where(lane == nz - 1, 0.0, pltpu.roll(v, nz - 1, 1))

    def down_z(v):
        return jnp.where(lane == 0, 0.0, pltpu.roll(v, 1, 1))

    def scale():
        value = red_src[0, 1]
        for k in range(1, ny):
            value = value + red_y[0, k - 1]
        return (ncells / value)[0:1]

    def forward(step):
        parts = [split(cur[c].reshape(rows, nz)) for c in range(comps)]
        stack = jnp.concatenate([p[0] for p in parts] + [p[1] for p in parts], axis=1)
        picked = mm(sel_t[...], stack).astype(BF16)
        data = jnp.zeros((1, 128), F32)
        for b in range(blocks):
            r = slice(16 * b, 16 * (b + 1))
            hi = jnp.concatenate([picked[r, nz * c : nz * (c + 1)] for c in range(comps)], axis=0)
            lo = jnp.concatenate([picked[r, nz * (comps + c) : nz * (comps + c + 1)] for c in range(comps)], axis=0)
            q = folded(hi, lo, w_ahead[b])
            u = uv[b]
            alive = iota((1, 128), 1) < fill_ref[b]
            back = []
            for c in range(comps):
                v = jnp.sum(q[16 * c : 16 * (c + 1)] * u, axis=0, keepdims=True)
                mis = jnp.where(alive, v - targ_ref[c : c + 1, 128 * b : 128 * (b + 1)], 0.0)
                data = data + mis * mis
                back.append((mis * 2.0) * u)
            dhi, dlo = split(jnp.concatenate(back, axis=0))
            t = folded(dhi, dlo, w_back[b])
            thi, tlo = split(t)
            for c in range(comps):
                term[r, nz * c : nz * (c + 1)] = thi[16 * c : 16 * (c + 1)]
                term[r, nz * (comps + c) : nz * (comps + c + 1)] = tlo[16 * c : 16 * (c + 1)]
        pulled = mm(sel[...], term[...])

        @pl.when(step == 0)
        def _():
            reduce_wait(0, 1)

        ratio = scale()
        spread = jnp.zeros((ey, nz), F32)
        div = []
        for x in range(1, cx + 1):
            one, two = cur[1, x], cur[2, x]
            dv = (cur[0, x + 1] - cur[0, x - 1] + up_y(one) - down_y(one) + up_z(two) - down_z(two)) / 2.0
            dv = jnp.where(own_y, dv, 0.0)
            spread = spread + dv * dv
            div.append(dv)
        for c in range(comps):
            whole = ratio * (pulled[:, nz * c : nz * (c + 1)] + pulled[:, nz * (comps + c) : nz * (comps + c + 1)])
            for x in range(ex):
                value = whole[ey * x : ey * (x + 1)]
                if c == 0:
                    if 0 <= x - 2 < cx:
                        value = value + penalty_weight * div[x - 2]
                    if x < cx:
                        value = value - penalty_weight * div[x]
                elif 1 <= x <= cx:
                    dv = div[x - 1]
                    if c == 1:
                        value = value + penalty_weight * (down_y(dv) - up_y(dv))
                    else:
                        value = value + penalty_weight * (down_z(dv) - up_z(dv))
                grad[c, x] = value
        return data * (ratio / ncells) + (penalty_weight / ncells) * jnp.sum(spread, axis=0, keepdims=True)

    def update(step):
        def pick(values):
            out = jnp.float32(values[-1])
            for i in range(ITERS - 1):
                out = jnp.where(step == i, jnp.float32(values[i]), out)
            return out
        rate = pick([learn_rate / (1.0 - beta_one ** (i + 1)) for i in range(ITERS)])
        corr = pick([1.0 / (1.0 - beta_two ** (i + 1)) for i in range(ITERS)])
        for c in range(comps):
            for x in range(ex):
                g = total[c, x] * mask_y
                if mask_x[x] is not None:
                    g = g * mask_x[x]
                m = beta_one * mom[c, x] + (1.0 - beta_one) * g
                s = beta_two * sec[c, x] + (1.0 - beta_two) * g * g
                mom[c, x], sec[c, x] = m, s
                cur[c, x] = cur[c, x] - (rate * m) / (jnp.sqrt(s * corr) + adam_eps)

    def body(step, losses):
        loss = forward(step)
        losses = jnp.where(sub == step, loss, losses)

        @pl.when(step == ITERS - 1)
        def _():
            reduce_start(1, 0, losses)

        send_faces(step + 1)

        @pl.when(step == ITERS - 1)
        def _():
            reduce_start(1, 1, reduce_wait(1, 0))

        recv_faces(step + 1)

        update(step)
        wait_sends(step + 1)
        return losses

    lax.fori_loop(0, ITERS, body, jnp.zeros((8, nz), F32))
    out_ref[...] = cur[:, 1 : cx + 1, 0:cy, :]
    final = reduce_wait(1, 1)
    for i in range(ITERS):
        loss_ref[i] = jnp.sum(final[i : i + 1])


def shards(nx, ny, coefficients, fractions, targets, block_cell, block_fill):
    comps, cx, cy, nz = coefficients.shape
    blocks = block_cell.shape[0]
    ex, ey = cx + 3, cy + 8
    rows = ex * ey
    state = pltpu.VMEM((comps, ex, ey, nz), F32)
    smem = pl.BlockSpec(memory_space=pltpu.SMEM)
    vmem = pl.BlockSpec(memory_space=pltpu.VMEM)
    dma = pltpu.SemaphoreType.DMA
    slots = ITERS + 1
    return pl.pallas_call(
        functools.partial(kernel, nx, ny),
        out_shape=(
            jax.ShapeDtypeStruct(coefficients.shape, F32),
            jax.ShapeDtypeStruct((ITERS,), F32),
        ),
        in_specs=[pl.BlockSpec(memory_space=pltpu.HBM)] * 5,
        out_specs=(vmem, smem),
        scratch_shapes=[
            pltpu.SMEM((blocks,), jnp.int32),
            pltpu.SMEM((blocks,), jnp.int32),
            pltpu.VMEM(coefficients.shape, F32),
            pltpu.VMEM(fractions.shape, F32),
            pltpu.VMEM(targets.shape, F32),
            dma((5,)),
            state, state, state, state, state,
            pltpu.VMEM((blocks, 2 * nz, 256), BF16),
            pltpu.VMEM((blocks, 256, 2 * nz), BF16),
            pltpu.VMEM((blocks, 16, 128), F32),
            pltpu.VMEM((rows, 16 * blocks), BF16),
            pltpu.VMEM((16 * blocks, rows), BF16),
            pltpu.VMEM((16 * blocks, 2 * comps * nz), BF16),
            pltpu.VMEM((2, 3 * comps, 8, nz), F32),
            pltpu.VMEM((4, 5, 8, nz), F32),
            pltpu.VMEM((slots, 2, comps, 3, ey, nz), F32),
            pltpu.VMEM((slots, 2, 3 * comps, 8, nz), F32),
            pltpu.VMEM((slots, 4, 5, 8, nz), F32),
            pltpu.VMEM((2, 2, 8, nz), F32),
            pltpu.VMEM((2, nx - 1, 8, nz), F32),
            pltpu.VMEM((2, ny - 1, 8, nz), F32),
            dma((slots, 8)), dma((slots, 8)),
            dma((2, nx - 1)), dma((2, nx - 1)),
            dma((2, ny - 1)), dma((2, ny - 1)),
        ],
        compiler_params=pltpu.CompilerParams(
            collective_id=0, has_side_effects=True, vmem_limit_bytes=60 * 1024 * 1024
        ),
    )(block_cell, block_fill, coefficients, fractions, targets)


def solution(mesh):
    nx, ny = mesh.shape["gx"], mesh.shape["gy"]
    return jax.shard_map(
        functools.partial(shards, nx, ny),
        mesh=mesh,
        in_specs=(
            P(None, "gx", "gy", None),
            P(None, ("gx", "gy")),
            P(None, ("gx", "gy")),
            P(("gx", "gy")),
            P(("gx", "gy")),
        ),
        out_specs=(P(None, "gx", "gy", None), P()),
        check_vma=False,
    )
```
